32 devices in a mesh: groups: 2 (over y), rows: 4 (over z), edges: 2 (over x), cols: 2 (over core).
Axes of the slice: x: 2, y: 2, z: 4, core: 2. Of those that a mesh axis runs over, the one named last changes fastest.
Arguments:
- entities: float32 [16384, 400], P(('groups', 'rows'), 'cols'), parts along dimension 0, may hold values from -1.8 to 1.8
- entity_state: float32 [16384], P(('groups', 'rows')), parts along dimension 0, may hold values from 0.001 to 0.01
- relations: float32 [6144, 400], P('groups', 'cols'), parts along dimension 0, may hold values from -6 to 6
- relation_state: float32 [6144], P('groups'), parts along dimension 0, may hold values from 0.001 to 0.01
- requests: int32 [8, 4, 2, 2, 64], P(('groups', 'rows'), None, 'edges'), parts along dimension 0, may hold values from -1 to 2047, as said below
- head_slot: int32 [8, 2, 2, 1024], P(('groups', 'rows'), 'edges', None, 'cols'), parts along dimension 0, may hold values from 0 to 255, as said below
- tail_slot: int32 [8, 2, 2, 1024], P(('groups', 'rows'), 'edges', None, 'cols'), parts along dimension 0, may hold values from 0 to 255, as said below
- relation_ids: int32 [8, 2, 2, 1024], P(('groups', 'rows'), 'edges', None, 'cols'), parts along dimension 0, may hold values from 0 to 3071
- negative_slot: int32 [8, 2, 2, 1536], P(('groups', 'rows'), 'edges'), parts along dimension 0, may hold values from 0 to 255, as said below
Outputs:
- new_entities: float32 [16384, 400], P(('groups', 'rows'), 'cols'), parts along dimension 0
- new_entity_state: float32 [16384], P(('groups', 'rows')), parts along dimension 0
- new_relations: float32 [6144, 400], P('groups', 'cols'), parts along dimension 0
- new_relation_state: float32 [6144], P('groups'), parts along dimension 0
The draws below stay inside these ranges and needn't reach their ends.
There are 2 independent parts, one for each index of `groups`. The reference program is written for one: setup_inputs(seed, part) draws one part's arguments, and reference() takes and returns one part's arrays. A program takes and returns all parts, laid end to end along the dimension named above; each array names one. Nothing has to cross between parts.
Inputs may be any that keep to these rules, and one draw needn't show every extreme that they name: requests[o, r, e, k, j] is a row of shard o or -1 for an empty slot; the ids of one list are distinct and the live ones come first; every list holds 16 or more live ids, and for each worker and block the list of one owner is full. `head_slot`: each value is o * 64 + j with j below the number of live ids in owner o's list for that worker and block. `tail_slot`: each value is o * 64 + j with j below the number of live ids in owner o's list for that worker and block. `negative_slot`: each value is o * 64 + j with j below the number of live ids in owner o's list for that worker and block.
All inputs are finite; a program needn't handle non-finite values.
Results may differ from the reference program's by a relative error of at most 0.0031.
Values may be sent and summed in bfloat16 or wider, within the bound.
A program may use at most 128 MiB of HBM per device.

```python
import math
import jax
import jax.numpy as jnp
import numpy as np
from jax import lax

W = 400
REL = 3072
ENT_DEV = 2048
SPANS = 2
SPAN = 1024
NEG = 1536
CAP = 64
ENT = 8192
N_ROWS = 4
N_EDGES = 2


def list_counts(key):
    key = jax.random.fold_in(key, 500)
    count_key, hot_key = jax.random.split(key)
    counts = jax.random.randint(count_key, (N_ROWS, N_EDGES, SPANS, N_ROWS), CAP // 4, CAP + 1)
    hottest = jax.random.randint(hot_key, (N_ROWS, N_EDGES, SPANS, 1), 0, N_ROWS)
    owners = jnp.arange(N_ROWS, dtype=jnp.int32)
    return jnp.where(owners == hottest, CAP, counts).astype(jnp.int32)


def pick_slots(counts, key, length):
    owner_key, place_key = jax.random.split(key)
    owners = jax.random.randint(owner_key, (N_ROWS, N_EDGES, SPANS, length), 0, N_ROWS)
    limits = jnp.take_along_axis(counts, owners, axis=3)
    places = jax.random.randint(place_key, owners.shape, 0, limits)
    return (owners * CAP + places).astype(jnp.int32)


def draw_requests(key, part):
    counts = list_counts(key)
    key = jax.random.fold_in(key, 1)
    block_total = N_ROWS * N_EDGES * SPANS * N_ROWS
    block_keys = jax.random.split(key, block_total)
    chosen = jax.vmap(lambda single: jax.random.permutation(single, ENT_DEV)[:CAP])(block_keys)
    chosen = chosen.reshape(N_ROWS, N_EDGES, SPANS, N_ROWS, CAP).astype(jnp.int32)
    live_mask = jnp.arange(CAP, dtype=jnp.int32) < counts[..., None]
    listed = jnp.where(live_mask, chosen, -1)
    return jnp.transpose(listed, (3, 0, 1, 2, 4)).astype(jnp.int32)


def draw_head_slot(key, part):
    counts = list_counts(key)
    key = jax.random.fold_in(key, 2)
    return pick_slots(counts, key, SPAN)


def draw_tail_slot(key, part):
    counts = list_counts(key)
    key = jax.random.fold_in(key, 3)
    return pick_slots(counts, key, SPAN)


def draw_negative_slot(key, part):
    counts = list_counts(key)
    key = jax.random.fold_in(key, 4)
    return pick_slots(counts, key, NEG)


def set_ends(values, stream_key, least, top_value):
    place = [jax.random.randint(jax.random.fold_in(stream_key, axis), (), 0, length) for axis, length in enumerate(values.shape)]
    main_axis = values.shape.index(max(values.shape))
    neighbour = place[:main_axis] + [(place[main_axis] + 1) % values.shape[main_axis]] + place[main_axis + 1:]
    return values.at[tuple(place)].set(least).at[tuple(neighbour)].set(top_value)


def level_of(key, extent, cuts, smallest, high):
    gain = 1.0
    for dim, shards_of in cuts:
        draws = jax.random.uniform(jax.random.fold_in(jax.random.fold_in(key, 6), dim), (shards_of,), jnp.float32, smallest / len(cuts), high / len(cuts))
        gain = gain * jnp.repeat(jnp.exp(draws), extent[dim] // shards_of).reshape((-1,) + (1,) * (len(extent) - 1 - dim))
    return gain


def rank_table(number_of, skew):
    weights = [(1 << 20) // math.isqrt(rank ** skew) + 1 for rank in range(1, number_of + 1)]
    scale = 1 + sum(weights) // (1 << 30)
    return np.cumsum(np.array([max(1, weight // scale) for weight in weights]))


def ranked_ids(stream_key, shape, amount, slope):
    listing = rank_table(amount, slope)
    pick = jax.random.randint(jax.random.fold_in(stream_key, 1), shape, 0, int(listing[amount - 1]))
    grade = jnp.searchsorted(jnp.asarray(listing, jnp.int32), pick, side="right")
    return jax.random.permutation(jax.random.fold_in(stream_key, 2), amount)[grade].astype(jnp.int32)


def bell_draw(own_key, extent, spread, most, shards=(), kind=jnp.bfloat16):
    entries = spread * jax.random.normal(own_key, extent, jnp.float32)
    if shards:
        entries = entries * level_of(own_key, extent, shards, -0.22, 0.18)
    return jnp.clip(entries, -most, most).astype(kind)


def setup_inputs(seed: int = 0, part: int = 0) -> dict:
    splits = jax.random.split(jax.random.key(seed), 10)
    own_keys = jax.random.split(jax.random.fold_in(splits[9], part), 10)
    entities = bell_draw(own_keys[0], (ENT, W), 0.3, 1.8, ((0, 4), (1, 2)), jnp.float32)
    entity_state = jnp.clip(jnp.exp(math.log(0.01) - 2.30258502 * jax.random.uniform(own_keys[1], (ENT,), jnp.float32) ** level_of(own_keys[1], (ENT,), ((0, 4),), -0.2, 0.2)), 0.001, 0.01)
    relations = bell_draw(own_keys[2], (REL, W), 1.0, 6.0, ((1, 2),), jnp.float32)
    relation_state = jnp.clip(jnp.exp(jax.random.uniform(own_keys[3], (REL,), jnp.float32, math.log(0.001), math.log(0.01))), 0.001, 0.01)
    requests = draw_requests(jax.random.fold_in(jax.random.fold_in(splits[9], part), 71), part)
    head_slot = draw_head_slot(jax.random.fold_in(jax.random.fold_in(splits[9], part), 71), part)
    tail_slot = draw_tail_slot(jax.random.fold_in(jax.random.fold_in(splits[9], part), 71), part)
    relation_ids = set_ends(ranked_ids(own_keys[7], (N_ROWS, N_EDGES, SPANS, SPAN), REL, 2), jax.random.fold_in(own_keys[7], 3), 0, REL - 1).astype(jnp.int32)
    negative_slot = draw_negative_slot(jax.random.fold_in(jax.random.fold_in(splits[9], part), 71), part)
    return dict(entities=entities, entity_state=entity_state, relations=relations, relation_state=relation_state, requests=requests, head_slot=head_slot, tail_slot=tail_slot, relation_ids=relation_ids, negative_slot=negative_slot)


LEARNING = 0.3

def complex_product(multiplier, multiplicand):
    mult_re = multiplier[..., 0::2]
    mult_im = multiplier[..., 1::2]
    cand_re = multiplicand[..., 0::2]
    cand_im = multiplicand[..., 1::2]
    real_part = mult_re * cand_re - mult_im * cand_im
    imag_part = mult_re * cand_im + mult_im * cand_re
    return jnp.stack([real_part, imag_part], axis=-1).reshape(multiplier.shape)

def conj_product(multiplier, multiplicand):
    mult_re = multiplier[..., 0::2]
    mult_im = multiplier[..., 1::2]
    cand_re = multiplicand[..., 0::2]
    cand_im = multiplicand[..., 1::2]
    real_part = mult_re * cand_re + mult_im * cand_im
    imag_part = mult_im * cand_re - mult_re * cand_im
    return jnp.stack([real_part, imag_part], axis=-1).reshape(multiplier.shape)

def edge_terms(fetched, relation_b, head_pick, tail_pick, relation_pick, negative_pick):
    head_rows = fetched[head_pick].astype(jnp.float32)
    tail_rows = fetched[tail_pick].astype(jnp.float32)
    relation_rows = relation_b[relation_pick].astype(jnp.float32)
    negative_rows = fetched[negative_pick]
    query = complex_product(head_rows, relation_rows)
    query_b = query.astype(jnp.bfloat16)
    positive = lax.optimization_barrier(jnp.sum(query * tail_rows, axis=1))
    scores = lax.dot_general(query_b, negative_rows, (((1,), (1,)), ((), ())), preferred_element_type=jnp.float32)
    pos_weight = -jax.nn.sigmoid(-positive)
    neg_weight = (jax.nn.sigmoid(scores) / negative_pick.shape[0]).astype(jnp.bfloat16)
    query_grad = pos_weight[:, None] * tail_rows + jnp.dot(neg_weight, negative_rows, preferred_element_type=jnp.float32)
    negative_grad = lax.dot_general(neg_weight, query_b, (((0,), (0,)), ((), ())), preferred_element_type=jnp.float32)
    tail_grad = pos_weight[:, None] * query
    head_grad = conj_product(query_grad, relation_rows)
    rho_grad = conj_product(query_grad, head_rows)
    slot_grad = jnp.zeros(fetched.shape, jnp.float32)
    slot_grad = slot_grad.at[head_pick].add(head_grad)
    slot_grad = slot_grad.at[tail_pick].add(tail_grad)
    slot_grad = slot_grad.at[negative_pick].add(negative_grad)
    return (slot_grad, rho_grad)

def reference(entities, entity_state, relations, relation_state, requests, head_slot, tail_slot, relation_ids, negative_slot):
    relation_b = relations.astype(jnp.bfloat16)
    owner_base = (jnp.arange(N_ROWS, dtype=jnp.int32) * ENT_DEV)[:, None]

    def one_block(carry, block_index):
        entity_grad, relation_grad = carry
        worker = block_index // (N_EDGES * SPANS)
        replica = block_index // SPANS % N_EDGES
        step_index = block_index % SPANS
        wanted = requests[:, worker, replica, step_index, :]
        live_mask = (wanted >= 0).reshape(-1, 1)
        global_rows = (owner_base + jnp.maximum(wanted, 0)).reshape(-1).astype(jnp.int32)
        fetched = jnp.where(live_mask, entities[global_rows], 0.0).astype(jnp.bfloat16)
        relation_pick = relation_ids[worker, replica, step_index]
        slot_grad, rho_grad = edge_terms(fetched, relation_b, head_slot[worker, replica, step_index], tail_slot[worker, replica, step_index], relation_pick, negative_slot[worker, replica, step_index])
        entity_grad = entity_grad.at[global_rows].add(jnp.where(live_mask, slot_grad, 0.0))
        relation_grad = relation_grad.at[relation_pick].add(rho_grad)
        return ((entity_grad, relation_grad), None)
    initial = (jnp.zeros(entities.shape, jnp.float32), jnp.zeros(relations.shape, jnp.float32))
    totals, unused = lax.scan(one_block, initial, jnp.arange(N_ROWS * N_EDGES * SPANS, dtype=jnp.int32))
    entity_grad, relation_grad = totals
    new_entity_state = entity_state + lax.optimization_barrier(jnp.sum(entity_grad * entity_grad, axis=1)) / W
    new_entities = entities - LEARNING * entity_grad / jnp.sqrt(new_entity_state)[:, None]
    new_relation_state = relation_state + lax.optimization_barrier(jnp.sum(relation_grad * relation_grad, axis=1)) / W
    new_relations = relations - LEARNING * relation_grad / jnp.sqrt(new_relation_state)[:, None]
    return (new_entities, new_entity_state, new_relations, new_relation_state)
```

```python
import functools

import jax
import jax.numpy as jnp
from jax import lax
from jax.experimental import pallas as pl
from jax.experimental.pallas import tpu as pltpu
from jax.sharding import PartitionSpec as P

LEARNING = 0.3
F32 = jnp.float32
BF16 = jnp.bfloat16
NT = (((1,), (1,)), ((), ()))
TN = (((0,), (0,)), ((), ()))


def dot(a, b):
    return jnp.dot(a, b, preferred_element_type=F32)


def dot_nt(a, b):
    return lax.dot_general(a, b, NT, preferred_element_type=F32)


def dot_tn(a, b):
    return lax.dot_general(a, b, TN, preferred_element_type=F32)


def one_hot(start, count, ids):
    rows = lax.broadcasted_iota(jnp.int32, (count, ids.shape[1]), 0) + start
    return jnp.where(rows == ids, 1.0, 0.0).astype(BF16)


def neighbours(x):
    grouped = x.reshape(x.shape[0] // 8, 8, x.shape[1])
    after = pltpu.roll(grouped, 7, 1).reshape(x.shape)
    before = pltpu.roll(grouped, 1, 1).reshape(x.shape)
    return after, before


def split_high(x):
    high = x.astype(BF16)
    return high, (x - high.astype(F32)).astype(BF16)


def pad_rows(x, rows):
    return jnp.concatenate([x, jnp.zeros((rows - x.shape[0], x.shape[1]), x.dtype)], axis=0)


def when(static, condition):
    if static:
        return lambda body: body()
    return pl.when(condition)


def kernel(
    n, ent, est, rel, rst, req, head, tail, rid, neg,
    new_ent, new_est, new_rel, new_rst,
    relb, entb, fetg, fet, allreq, oh_head, oh_tail, oh_rel, share, rho, rho_hi, rho_lo,
    slot_grad, ent_send, ent_in, grad_out, grad_in, sq_ent, sq_ent_in,
    pair_out, pair_in, pair_sum, x_out, x_in, z_out, z_in, total, sq_rel, sq_rel_in,
    s_relb, r_relb, s_req, r_req, s_fet, r_fet, s_ent, r_ent, s_grad, r_grad,
    s_pair, r_pair, s_x, r_x, s_z, r_z, s_agz, r_agz, s_agx, r_agx, s_sq, r_sq,
):
    R, E, K, PW, L, PIECES, HP = n.rows, n.edges, n.blocks, n.width, n.lanes, n.pieces, n.padded
    r, e, c = lax.axis_index("rows"), lax.axis_index("edges"), lax.axis_index("cols")
    pc = 1 - c
    half = ent.shape[0]
    full = PIECES == R

    def remote(src, dst, s_sem, r_sem, row, edge, col):
        return pltpu.make_async_remote_copy(
            src_ref=src, dst_ref=dst, send_sem=s_sem, recv_sem=r_sem,
            device_id={"rows": row, "edges": edge, "cols": col},
            device_id_type=pl.DeviceIdType.MESH,
        )

    barrier = pltpu.get_barrier_semaphore()
    for dr in range(R):
        for de in range(E):
            for dc in range(2):
                if dr or de or dc:
                    pl.semaphore_signal(
                        barrier, inc=1,
                        device_id={
                            "rows": lax.rem(r + dr, R),
                            "edges": lax.rem(e + de, E),
                            "cols": lax.rem(c + dc, 2),
                        },
                        device_id_type=pl.DeviceIdType.MESH,
                    )
    sent = []

    entb[...] = pad_rows(ent[...], HP).astype(BF16)
    relb[c] = pad_rows(rel[...], HP).astype(BF16)
    allreq[e] = req[...]
    for w in range(R):
        ids = req[:, w * PW : (w + 1) * PW]
        fetg[w] = dot(entb[...], one_hot(0, ent.shape[1], ids)).astype(BF16)
    pl.semaphore_wait(barrier, R * E * 2 - 1)

    fetch = []
    for dr in range(R):
        row = lax.rem(r + dr, R)
        here = fet.at[c, :, pl.ds(pl.multiple_of(r * PW, PW), PW)]
        for dc in range(2):
            if dr or dc:
                i = dr * 2 + dc - 1
                copy = remote(fetg.at[row], here, s_fet.at[i], r_fet.at[i], row, e, lax.rem(c + dc, 2))
                copy.start()
                fetch.append(copy)
    fet[c, :, pl.ds(pl.multiple_of(r * PW, PW), PW)] = fetg[r]
    relation_copy = remote(relb.at[c], relb.at[c], s_relb.at[0], r_relb.at[0], r, e, pc)
    relation_copy.start()
    request_copies = []
    for de in range(1, E):
        copy = remote(
            allreq.at[e], allreq.at[e], s_req.at[de - 1], r_req.at[de - 1], r, lax.rem(e + de, E), c
        )
        copy.start()
        request_copies.append(copy)
    sent += fetch + [relation_copy] + request_copies

    positions = R * PW
    negatives = neg.shape[1] // K
    for k in range(K):
        slots = lax.broadcasted_iota(jnp.int32, (positions, 128), 0)
        hits = jnp.zeros((positions, 128), F32)
        for at in range(k * negatives, (k + 1) * negatives, 128):
            hits += jnp.where(slots == neg[:, at : at + 128], 1.0, 0.0)
        share[k] = jnp.sum(hits, axis=1, keepdims=True) / negatives

    edges = head.shape[1]
    step = n.step

    @pl.loop(0, edges // step)
    def _(t):
        cols = pl.ds(pl.multiple_of(t * step, step), step)
        oh_head[:, cols] = one_hot(0, positions, head[:, cols])
        oh_tail[:, cols] = one_hot(0, positions, tail[:, cols])
        oh_rel[:, cols] = one_hot(0, rel.shape[1], rid[:, cols])
        rho[c, :, cols] = dot(relb[c], oh_rel[:, cols]).astype(BF16)

    relation_copy.wait_recv()

    @pl.loop(0, edges // step)
    def _(t):
        cols = pl.ds(pl.multiple_of(t * step, step), step)
        rho[pc, :, cols] = dot(relb[pc], oh_rel[:, cols]).astype(BF16)

    for copy in fetch:
        copy.wait_recv()

    slot_grad[...] = jnp.zeros_like(slot_grad)
    per_block = edges // K
    for k in range(K):

        @pl.loop(0, per_block // step)
        def _(t):
            cols = pl.ds(pl.multiple_of(k * per_block + t * step, step), step)
            rows = fet[...].reshape(2 * HP, positions)
            h = dot(rows, oh_head[:, cols])
            tl = dot(rows, oh_tail[:, cols])
            rh = rho[:, :, cols].reshape(2 * HP, step).astype(F32)
            even = lax.rem(lax.broadcasted_iota(jnp.int32, (2 * HP, step), 0), 2) == 0
            h_after, h_before = neighbours(h)
            r_after, r_before = neighbours(rh)
            r_re = jnp.where(even, rh, r_before)
            r_im = jnp.where(even, -r_after, rh)
            query = h * r_re + jnp.where(even, h_after, h_before) * r_im
            query_b = query.astype(BF16)
            positive = jnp.sum(query * tl, axis=0, keepdims=True)
            pos_weight = -jax.nn.sigmoid(-positive)
            scores = dot_tn(rows, query_b)
            weight = (jax.nn.sigmoid(scores) * share[k]).astype(BF16)
            g = pos_weight * tl + dot(rows, weight)
            g_after, g_before = neighbours(g)
            g_swap = jnp.where(even, g_after, g_before)
            head_grad = g * r_re - g_swap * r_im
            h_re = jnp.where(even, h, h_before)
            h_im = jnp.where(even, -h_after, h)
            rho_grad = g * h_re - g_swap * h_im
            high, low = split_high(rho_grad)
            rho_hi[:, :, cols] = high.reshape(2, HP, step)
            rho_lo[:, :, cols] = low.reshape(2, HP, step)
            acc = dot_nt(query_b, weight)
            high, low = split_high(head_grad)
            acc += dot_nt(high, oh_head[:, cols]) + dot_nt(low, oh_head[:, cols])
            high, low = split_high(pos_weight * query)
            acc += dot_nt(high, oh_tail[:, cols]) + dot_nt(low, oh_tail[:, cols])
            slot_grad[...] += acc.reshape(2, HP, positions)

    ent_send[...] = slot_grad[pc]
    entity_pair = remote(ent_send, ent_in, s_ent.at[0], r_ent.at[0], r, e, pc)
    entity_pair.start()
    sent.append(entity_pair)

    def place(de, p):
        return pl.multiple_of((lax.rem(e + de, E) * PIECES + p) * L, L)

    order = [(de, p) for de in list(range(1, E)) + [0] for p in range(PIECES)]
    pairs = {}

    def dense(which, de, p):
        hot = oh_rel[pl.ds(place(de, p), L), :]
        return dot_nt(rho_hi[which], hot) + dot_nt(rho_lo[which], hot)

    def send_pair(de, p):
        i = de * PIECES + p
        pair_out[i] = dense(pc, de, p)
        copy = remote(pair_out.at[i], pair_in.at[i], s_pair.at[i], r_pair.at[i], r, e, pc)
        copy.start()
        pairs[de, p] = copy
        sent.append(copy)

    def x_copy(de, p):
        i = (de - 1) * PIECES + p
        return remote(x_out.at[i], x_in.at[i], s_x.at[i], r_x.at[i], r, lax.rem(e + de, E), c)

    def entity_out():
        entity_pair.wait_recv()
        summed = (slot_grad[c] + ent_in[...]).astype(BF16)
        for o in range(R):
            grad_out[o] = summed[:, o * PW : (o + 1) * PW]
        copies = []
        for dr in range(R):
            row = lax.rem(r + dr, R)
            for de in range(E):
                if dr or de:
                    i = dr * E + de - 1
                    copy = remote(
                        grad_out.at[row],
                        grad_in.at[e, :, pl.ds(pl.multiple_of(r * PW, PW), PW)],
                        s_grad.at[i], r_grad.at[i], row, lax.rem(e + de, E), c,
                    )
                    copy.start()
                    copies.append(copy)
        grad_in[e, :, pl.ds(pl.multiple_of(r * PW, PW), PW)] = grad_out[r]
        sent.extend(copies)
        return copies

    send_pair(*order[0])
    for at, (de, p) in enumerate(order):
        if at + 1 < len(order):
            send_pair(*order[at + 1])
        own = dense(c, de, p)
        pairs[de, p].wait_recv()
        own += pair_in[de * PIECES + p]
        if de:
            x_out[(de - 1) * PIECES + p] = own.astype(BF16)
            copy = x_copy(de, p)
            copy.start()
            sent.append(copy)
        else:
            pair_sum[p] = own
    grads = entity_out()

    def over_edges(p):
        acc = pair_sum[p]
        for de in range(1, E):
            x_copy(de, p).wait_recv()
            acc += x_in[(de - 1) * PIECES + p].astype(F32)
        return acc

    def z_copy(dr):
        return remote(
            z_out.at[dr - 1], z_in.at[dr - 1], s_z.at[dr - 1], r_z.at[dr - 1], lax.rem(r + dr, R), e, c
        )

    for dr in range(1, R):
        p = lax.rem(r + dr, R)

        @when(full, p < PIECES)
        def _():
            z_out[dr - 1] = over_edges(p).astype(BF16)
            z_copy(dr).start()

    def mine(dr):
        return e * PIECES + lax.rem(r + R - dr, R)

    def agz_copy(dr):
        return remote(
            total.at[mine(0)], total.at[mine(0)], s_agz.at[dr - 1], r_agz.at[dr - 1],
            lax.rem(r + dr, R), e, c,
        )

    def agx_copy(dr, de):
        i = dr * (E - 1) + de - 1
        return remote(
            total.at[mine(dr)], total.at[mine(dr)], s_agx.at[i], r_agx.at[i],
            r, lax.rem(e + de, E), c,
        )

    @when(full, r < PIECES)
    def _():
        acc = over_edges(r)
        for dr in range(1, R):
            z_copy(dr).wait_recv()
            acc += z_in[dr - 1].astype(F32)
        total[mine(0)] = acc.astype(BF16)
        for dr in range(1, R):
            agz_copy(dr).start()
        for de in range(1, E):
            agx_copy(0, de).start()

    for copy in request_copies + grads:
        copy.wait_recv()
    tile = n.tile

    @pl.loop(0, ent.shape[1] // tile)
    def _(t):
        cols = pl.ds(pl.multiple_of(t * tile, tile), tile)
        acc = jnp.zeros((HP, tile), F32)
        for edge in range(E):
            acc += dot_nt(grad_in[edge], one_hot(t * tile, tile, allreq[edge]))
        new_ent[:, cols] = acc[:half, :]
        sq_ent[:, cols] = jnp.sum(acc * acc, axis=0, keepdims=True)

    squares = remote(sq_ent, sq_ent_in, s_sq.at[0], r_sq.at[0], r, e, pc)
    squares.start()
    sent.append(squares)

    for dr in range(1, R):

        @when(full, lax.rem(r + R - dr, R) < PIECES)
        def _():
            agz_copy(dr).wait_recv()
            for de in range(1, E):
                agx_copy(dr, de).start()

    squares.wait_recv()
    state = est[...] + (sq_ent[...] + sq_ent_in[...]) / (2 * half)
    new_est[...] = state
    new_ent[...] = ent[...] - new_ent[...] * (LEARNING / jnp.sqrt(state))

    for dr in range(R):
        for de in range(1, E):

            @when(full, lax.rem(r + R - dr, R) < PIECES)
            def _():
                agx_copy(dr, de).wait_recv()

    for i in range(E * PIECES):
        g = total[i].astype(F32)
        sq_rel[:, i * L : (i + 1) * L] = jnp.sum(g * g, axis=0, keepdims=True)
    squares = remote(sq_rel, sq_rel_in, s_sq.at[1], r_sq.at[1], r, e, pc)
    squares.start()
    sent.append(squares)
    squares.wait_recv()
    state = rst[...] + (sq_rel[...] + sq_rel_in[...]) / (2 * half)
    new_rst[...] = state
    scale = LEARNING / jnp.sqrt(state)
    for i in range(E * PIECES):
        at = slice(i * L, (i + 1) * L)
        new_rel[:, at] = rel[:, at] - total[i].astype(F32)[:half, :] * scale[:, at]

    for copy in sent:
        copy.wait_send()
    for dr in range(1, R):

        @when(full, lax.rem(r + dr, R) < PIECES)
        def _():
            z_copy(dr).wait_send()

        @when(full, r < PIECES)
        def _():
            agz_copy(dr).wait_send()

    for dr in range(R):
        for de in range(1, E):

            @when(full, lax.rem(r + R - dr, R) < PIECES)
            def _():
                agx_copy(dr, de).wait_send()


class Sizes:
    pass


def local(
    entities, entity_state, relations, relation_state, requests,
    head_slot, tail_slot, relation_ids, negative_slot,
):
    n = Sizes()
    n.rows, n.edges = lax.axis_size("rows"), lax.axis_size("edges")
    n.blocks = requests.shape[3]
    capacity = requests.shape[4]
    shard_rows, half = entities.shape
    types = relations.shape[0]
    n.width = n.blocks * capacity
    n.padded = -(-half // 16) * 16
    n.lanes = -(-types // (n.rows * n.edges * 128)) * 128
    n.pieces = types // (n.edges * n.lanes)
    n.step = 256 if n.rows * n.width <= 1024 else 128
    n.tile = 256
    positions = n.rows * n.width
    edges = n.blocks * head_slot.shape[3]

    def spots(slots):
        slots = slots[0, 0]
        block = jnp.arange(n.blocks, dtype=jnp.int32)[:, None]
        return ((slots // capacity) * n.width + block * capacity + slots % capacity).reshape(1, -1)

    HP, R, E, PC, L = n.padded, n.rows, n.edges, n.pieces, n.lanes
    V = pltpu.VMEM
    sem = lambda k: pltpu.SemaphoreType.DMA((max(k, 1),))
    scratch = [
        V((2, HP, types), BF16), V((HP, shard_rows), BF16), V((R, HP, n.width), BF16),
        V((2, HP, positions), BF16), V((E, 1, positions), jnp.int32),
        V((positions, edges), BF16), V((positions, edges), BF16), V((types, edges), BF16),
        V((n.blocks, positions, 1), F32), V((2, HP, edges), BF16),
        V((2, HP, edges), BF16), V((2, HP, edges), BF16),
        V((2, HP, positions), F32), V((HP, positions), F32), V((HP, positions), F32),
        V((R, HP, n.width), BF16), V((E, HP, positions), BF16),
        V((1, shard_rows), F32), V((1, shard_rows), F32),
        V((E * PC, HP, L), F32), V((E * PC, HP, L), F32), V((PC, HP, L), F32),
        V((max((E - 1) * PC, 1), HP, L), BF16), V((max((E - 1) * PC, 1), HP, L), BF16),
        V((max(R - 1, 1), HP, L), BF16), V((max(R - 1, 1), HP, L), BF16),
        V((E * PC, HP, L), BF16), V((1, types), F32), V((1, types), F32),
    ]
    for count in (1, E - 1, 2 * R - 1, 1, R * E - 1, E * PC, (E - 1) * PC, R - 1, R - 1, R * (E - 1), 2):
        scratch += [sem(count), sem(count)]
    vm = pl.BlockSpec(memory_space=pltpu.VMEM)
    new_ent, new_est, new_rel, new_rst = pl.pallas_call(
        functools.partial(kernel, n),
        out_shape=[
            jax.ShapeDtypeStruct((half, shard_rows), F32),
            jax.ShapeDtypeStruct((1, shard_rows), F32),
            jax.ShapeDtypeStruct((half, types), F32),
            jax.ShapeDtypeStruct((1, types), F32),
        ],
        in_specs=[vm] * 9,
        out_specs=[vm] * 4,
        scratch_shapes=scratch,
        compiler_params=pltpu.CompilerParams(
            collective_id=0, has_side_effects=True, vmem_limit_bytes=60 * 2**20
        ),
        name="complex_step",
    )(
        entities.T, entity_state.reshape(1, -1), relations.T, relation_state.reshape(1, -1),
        requests.reshape(1, -1), spots(head_slot), spots(tail_slot),
        relation_ids.reshape(1, -1), spots(negative_slot),
    )
    return new_ent.T, new_est.reshape(-1), new_rel.T, new_rst.reshape(-1)


def solution(mesh):
    placed = (
        P(("groups", "rows"), "cols"),
        P(("groups", "rows")),
        P("groups", "cols"),
        P("groups"),
        P(("groups", "rows"), None, "edges", None, None),
        P(("groups", "rows"), "edges", None, "cols"),
        P(("groups", "rows"), "edges", None, "cols"),
        P(("groups", "rows"), "edges", None, "cols"),
        P(("groups", "rows"), "edges", None, None),
    )
    return jax.shard_map(
        local,
        mesh=mesh,
        in_specs=placed,
        out_specs=(
            P(("groups", "rows"), "cols"),
            P(("groups", "rows")),
            P("groups", "cols"),
            P("groups"),
        ),
        check_vma=False,
    )
```

```python
import functools

import jax
import jax.numpy as jnp
from jax import lax
from jax.experimental import pallas as pl
from jax.experimental.pallas import tpu as pltpu
from jax.sharding import PartitionSpec as P

LEARNING = 0.3
F32 = jnp.float32
BF16 = jnp.bfloat16
NT = (((1,), (1,)), ((), ()))
TN = (((0,), (0,)), ((), ()))


def dot(a, b):
    return jnp.dot(a, b, preferred_element_type=F32)


def dot_nt(a, b):
    return lax.dot_general(a, b, NT, preferred_element_type=F32)


def dot_tn(a, b):
    return lax.dot_general(a, b, TN, preferred_element_type=F32)


def one_hot(start, count, ids):
    rows = lax.broadcasted_iota(jnp.int32, (count, ids.shape[1]), 0) + start
    return jnp.where(rows == ids, 1.0, 0.0).astype(BF16)


def neighbours(x):
    grouped = x.reshape(x.shape[0] // 8, 8, x.shape[1])
    after = pltpu.roll(grouped, 7, 1).reshape(x.shape)
    before = pltpu.roll(grouped, 1, 1).reshape(x.shape)
    return after, before


def positions_of(slots, k, capacity, width):
    if capacity & (capacity - 1):
        owner = lax.div(slots, jnp.full_like(slots, capacity))
    else:
        owner = lax.shift_right_logical(slots, jnp.full_like(slots, capacity.bit_length() - 1))
    return slots + owner * (width - capacity) + k * capacity


def pad_rows(x, rows):
    return jnp.concatenate([x, jnp.zeros((rows - x.shape[0], x.shape[1]), x.dtype)], axis=0)


def when(static, condition):
    if static:
        return lambda body: body()
    return pl.when(condition)


def kernel(
    n, ent, est, rel, rst, req, head, tail, rid, neg,
    new_ent, new_est, new_rel, new_rst,
    relb, entb, fetg, fet, allreq, oh_head, oh_tail, oh_rel, share, rho, rho_grads,
    slot_grad, ent_send, ent_in, grad_out, grad_in, sq_ent, sq_ent_in,
    pair_out, pair_in, pair_sum, x_out, x_in, z_out, z_in, total, sq_rel, sq_rel_in,
    s_relb, r_relb, s_req, r_req, s_fet, r_fet, s_ent, r_ent, s_grad, r_grad,
    s_pair, r_pair, s_x, r_x, s_z, r_z, s_agz, r_agz, s_agx, r_agx, s_sq, r_sq,
):
    R, E, K, PW, L, PIECES, HP = n.rows, n.edges, n.blocks, n.width, n.lanes, n.pieces, n.padded
    r, e, c = lax.axis_index("rows"), lax.axis_index("edges"), lax.axis_index("cols")
    pc = 1 - c
    half = ent.shape[0]
    full = PIECES == R

    def remote(src, dst, s_sem, r_sem, row, edge, col):
        return pltpu.make_async_remote_copy(
            src_ref=src, dst_ref=dst, send_sem=s_sem, recv_sem=r_sem,
            device_id={"rows": row, "edges": edge, "cols": col},
            device_id_type=pl.DeviceIdType.MESH,
        )

    barrier = pltpu.get_barrier_semaphore()
    for dr in range(R):
        for de in range(E):
            for dc in range(2):
                if dr or de or dc:
                    pl.semaphore_signal(
                        barrier, inc=1,
                        device_id={
                            "rows": lax.rem(r + dr, R),
                            "edges": lax.rem(e + de, E),
                            "cols": lax.rem(c + dc, 2),
                        },
                        device_id_type=pl.DeviceIdType.MESH,
                    )
    sent = []

    entb[...] = pad_rows(ent[...], HP).astype(BF16)
    relb[c] = pad_rows(rel[...], HP).astype(BF16)
    for w in range(R):
        ids = jnp.concatenate([req[w, k : k + 1, :] for k in range(K)], axis=1)
        allreq[e, :, w * PW : (w + 1) * PW] = ids
        fetg[w] = dot(entb[...], one_hot(0, ent.shape[1], ids)).astype(BF16)
    pl.semaphore_wait(barrier, R * E * 2 - 1)

    fetch = []
    for dr in range(R):
        row = lax.rem(r + dr, R)
        here = fet.at[c, :, pl.ds(pl.multiple_of(r * PW, PW), PW)]
        for dc in range(2):
            if dr or dc:
                i = dr * 2 + dc - 1
                copy = remote(fetg.at[row], here, s_fet.at[i], r_fet.at[i], row, e, lax.rem(c + dc, 2))
                copy.start()
                fetch.append(copy)
    fet[c, :, pl.ds(pl.multiple_of(r * PW, PW), PW)] = fetg[r]
    relation_copy = remote(relb.at[c], relb.at[c], s_relb.at[0], r_relb.at[0], r, e, pc)
    relation_copy.start()
    request_copies = []
    for de in range(1, E):
        copy = remote(
            allreq.at[e], allreq.at[e], s_req.at[de - 1], r_req.at[de - 1], r, lax.rem(e + de, E), c
        )
        copy.start()
        request_copies.append(copy)
    sent += fetch + [relation_copy] + request_copies

    positions = R * PW
    negatives = neg.shape[1]
    for k in range(K):
        slots = lax.broadcasted_iota(jnp.int32, (positions, 128), 0)
        hits = jnp.zeros((positions, 128), F32)
        for at in range(0, negatives, 128):
            ids = positions_of(neg[k : k + 1, at : at + 128], k, n.capacity, PW)
            hits += jnp.where(slots == ids, 1.0, 0.0)
        share[k] = jnp.sum(hits, axis=1, keepdims=True) / negatives

    per_block = head.shape[1]
    edges = K * per_block
    step = n.step
    for k in range(K):

        @pl.loop(0, per_block // step)
        def _(t):
            ids = pl.ds(pl.multiple_of(t * step, step), step)
            cols = pl.ds(pl.multiple_of(k * per_block + t * step, step), step)
            heads = positions_of(head[k : k + 1, ids], k, n.capacity, PW)
            tails = positions_of(tail[k : k + 1, ids], k, n.capacity, PW)
            oh_head[:, cols] = one_hot(0, positions, heads)
            oh_tail[:, cols] = one_hot(0, positions, tails)
            oh_rel[:, cols] = one_hot(0, rel.shape[1], rid[k : k + 1, ids])
            rho[c, :, cols] = dot(relb[c], oh_rel[:, cols]).astype(BF16)

    relation_copy.wait_recv()

    @pl.loop(0, edges // step)
    def _(t):
        cols = pl.ds(pl.multiple_of(t * step, step), step)
        rho[pc, :, cols] = dot(relb[pc], oh_rel[:, cols]).astype(BF16)

    for copy in fetch:
        copy.wait_recv()

    slot_grad[...] = jnp.zeros_like(slot_grad)
    for k in range(K):

        @pl.loop(0, per_block // step)
        def _(t):
            cols = pl.ds(pl.multiple_of(k * per_block + t * step, step), step)
            rows = fet[...].reshape(2 * HP, positions)
            h = dot(rows, oh_head[:, cols])
            tl = dot(rows, oh_tail[:, cols])
            rh = rho[:, :, cols].reshape(2 * HP, step).astype(F32)
            even = lax.rem(lax.broadcasted_iota(jnp.int32, (2 * HP, step), 0), 2) == 0
            h_after, h_before = neighbours(h)
            r_after, r_before = neighbours(rh)
            r_re = jnp.where(even, rh, r_before)
            r_im = jnp.where(even, -r_after, rh)
            query = h * r_re + jnp.where(even, h_after, h_before) * r_im
            query_b = query.astype(BF16)
            positive = jnp.sum(query * tl, axis=0, keepdims=True)
            pos_weight = -jax.nn.sigmoid(-positive)
            scores = dot_tn(rows, query_b)
            weight = (jax.nn.sigmoid(scores) * share[k]).astype(BF16)
            g = pos_weight * tl + dot(rows, weight)
            g_after, g_before = neighbours(g)
            g_swap = jnp.where(even, g_after, g_before)
            head_grad = g * r_re - g_swap * r_im
            h_re = jnp.where(even, h, h_before)
            h_im = jnp.where(even, -h_after, h)
            rho_grad = g * h_re - g_swap * h_im
            rho_grads[:, :, cols] = rho_grad.astype(BF16).reshape(2, HP, step)
            acc = dot_nt(query_b, weight)
            acc += dot_nt(head_grad.astype(BF16), oh_head[:, cols])
            acc += dot_nt((pos_weight * query).astype(BF16), oh_tail[:, cols])
            slot_grad[...] += acc.reshape(2, HP, positions)

    ent_send[...] = slot_grad[pc]
    entity_pair = remote(ent_send, ent_in, s_ent.at[0], r_ent.at[0], r, e, pc)
    entity_pair.start()
    sent.append(entity_pair)

    def place(de, p):
        return pl.multiple_of((lax.rem(e + de, E) * PIECES + p) * L, L)

    order = [(de, p) for de in list(range(1, E)) + [0] for p in range(PIECES)]
    pairs = {}

    def dense(which, de, p):
        hot = oh_rel[pl.ds(place(de, p), L), :]
        return dot_nt(rho_grads[which], hot)

    def send_pair(de, p):
        i = de * PIECES + p
        pair_out[i] = dense(pc, de, p)
        copy = remote(pair_out.at[i], pair_in.at[i], s_pair.at[i], r_pair.at[i], r, e, pc)
        copy.start()
        pairs[de, p] = copy
        sent.append(copy)

    def x_copy(de, p):
        i = (de - 1) * PIECES + p
        return remote(x_out.at[i], x_in.at[i], s_x.at[i], r_x.at[i], r, lax.rem(e + de, E), c)

    def entity_out():
        entity_pair.wait_recv()
        summed = (slot_grad[c] + ent_in[...]).astype(BF16)
        for o in range(R):
            grad_out[o] = summed[:, o * PW : (o + 1) * PW]
        copies = []
        for dr in range(R):
            row = lax.rem(r + dr, R)
            for de in range(E):
                if dr or de:
                    i = dr * E + de - 1
                    copy = remote(
                        grad_out.at[row],
                        grad_in.at[e, :, pl.ds(pl.multiple_of(r * PW, PW), PW)],
                        s_grad.at[i], r_grad.at[i], row, lax.rem(e + de, E), c,
                    )
                    copy.start()
                    copies.append(copy)
        grad_in[e, :, pl.ds(pl.multiple_of(r * PW, PW), PW)] = grad_out[r]
        sent.extend(copies)
        return copies

    send_pair(*order[0])
    for at, (de, p) in enumerate(order):
        if at + 1 < len(order):
            send_pair(*order[at + 1])
        own = dense(c, de, p)
        pairs[de, p].wait_recv()
        own += pair_in[de * PIECES + p]
        if de:
            x_out[(de - 1) * PIECES + p] = own.astype(BF16)
            copy = x_copy(de, p)
            copy.start()
            sent.append(copy)
        else:
            pair_sum[p] = own
    grads = entity_out()

    def over_edges(p):
        acc = pair_sum[p]
        for de in range(1, E):
            x_copy(de, p).wait_recv()
            acc += x_in[(de - 1) * PIECES + p].astype(F32)
        return acc

    def z_copy(dr):
        return remote(
            z_out.at[dr - 1], z_in.at[dr - 1], s_z.at[dr - 1], r_z.at[dr - 1], lax.rem(r + dr, R), e, c
        )

    for dr in range(1, R):
        p = lax.rem(r + dr, R)

        @when(full, p < PIECES)
        def _():
            z_out[dr - 1] = over_edges(p).astype(BF16)
            z_copy(dr).start()

    def mine(dr):
        return e * PIECES + lax.rem(r + R - dr, R)

    def agz_copy(dr):
        return remote(
            total.at[mine(0)], total.at[mine(0)], s_agz.at[dr - 1], r_agz.at[dr - 1],
            lax.rem(r + dr, R), e, c,
        )

    def agx_copy(dr, de):
        i = dr * (E - 1) + de - 1
        return remote(
            total.at[mine(dr)], total.at[mine(dr)], s_agx.at[i], r_agx.at[i],
            r, lax.rem(e + de, E), c,
        )

    @when(full, r < PIECES)
    def _():
        acc = over_edges(r)
        for dr in range(1, R):
            z_copy(dr).wait_recv()
            acc += z_in[dr - 1].astype(F32)
        total[mine(0)] = acc.astype(BF16)
        for dr in range(1, R):
            agz_copy(dr).start()
        for de in range(1, E):
            agx_copy(0, de).start()

    for copy in request_copies + grads:
        copy.wait_recv()
    tile = n.tile

    @pl.loop(0, ent.shape[1] // tile)
    def _(t):
        cols = pl.ds(pl.multiple_of(t * tile, tile), tile)
        acc = jnp.zeros((HP, tile), F32)
        for edge in range(E):
            acc += dot_nt(grad_in[edge], one_hot(t * tile, tile, allreq[edge]))
        new_ent[:, cols] = acc[:half, :]
        sq_ent[:, cols] = jnp.sum(acc * acc, axis=0, keepdims=True)

    squares = remote(sq_ent, sq_ent_in, s_sq.at[0], r_sq.at[0], r, e, pc)
    squares.start()
    sent.append(squares)

    for dr in range(1, R):

        @when(full, lax.rem(r + R - dr, R) < PIECES)
        def _():
            agz_copy(dr).wait_recv()
            for de in range(1, E):
                agx_copy(dr, de).start()

    squares.wait_recv()
    state = est[...] + (sq_ent[...] + sq_ent_in[...]) / (2 * half)
    new_est[...] = state
    new_ent[...] = ent[...] - new_ent[...] * (LEARNING / jnp.sqrt(state))

    for dr in range(R):
        for de in range(1, E):

            @when(full, lax.rem(r + R - dr, R) < PIECES)
            def _():
                agx_copy(dr, de).wait_recv()

    for i in range(E * PIECES):
        g = total[i].astype(F32)
        sq_rel[:, i * L : (i + 1) * L] = jnp.sum(g * g, axis=0, keepdims=True)
    squares = remote(sq_rel, sq_rel_in, s_sq.at[1], r_sq.at[1], r, e, pc)
    squares.start()
    sent.append(squares)
    squares.wait_recv()
    state = rst[...] + (sq_rel[...] + sq_rel_in[...]) / (2 * half)
    new_rst[...] = state
    scale = LEARNING / jnp.sqrt(state)
    for i in range(E * PIECES):
        at = slice(i * L, (i + 1) * L)
        new_rel[:, at] = rel[:, at] - total[i].astype(F32)[:half, :] * scale[:, at]

    for copy in sent:
        copy.wait_send()
    for dr in range(1, R):

        @when(full, lax.rem(r + dr, R) < PIECES)
        def _():
            z_copy(dr).wait_send()

        @when(full, r < PIECES)
        def _():
            agz_copy(dr).wait_send()

    for dr in range(R):
        for de in range(1, E):

            @when(full, lax.rem(r + R - dr, R) < PIECES)
            def _():
                agx_copy(dr, de).wait_send()


class Sizes:
    pass


def local(
    entities, entity_state, relations, relation_state, requests,
    head_slot, tail_slot, relation_ids, negative_slot,
):
    n = Sizes()
    n.rows, n.edges = lax.axis_size("rows"), lax.axis_size("edges")
    n.blocks = requests.shape[3]
    capacity = n.capacity = requests.shape[4]
    shard_rows, half = entities.shape
    types = relations.shape[0]
    n.width = n.blocks * capacity
    n.padded = -(-half // 16) * 16
    n.lanes = -(-types // (n.rows * n.edges * 128)) * 128
    n.pieces = types // (n.edges * n.lanes)
    n.step = 256 if n.rows * n.width <= 1024 else 128
    n.tile = 256
    positions = n.rows * n.width
    edges = n.blocks * head_slot.shape[3]

    HP, R, E, PC, L = n.padded, n.rows, n.edges, n.pieces, n.lanes
    V = pltpu.VMEM
    sem = lambda k: pltpu.SemaphoreType.DMA((max(k, 1),))
    scratch = [
        V((2, HP, types), BF16), V((HP, shard_rows), BF16), V((R, HP, n.width), BF16),
        V((2, HP, positions), BF16), V((E, 1, positions), jnp.int32),
        V((positions, edges), BF16), V((positions, edges), BF16), V((types, edges), BF16),
        V((n.blocks, positions, 1), F32), V((2, HP, edges), BF16),
        V((2, HP, edges), BF16),
        V((2, HP, positions), F32), V((HP, positions), F32), V((HP, positions), F32),
        V((R, HP, n.width), BF16), V((E, HP, positions), BF16),
        V((1, shard_rows), F32), V((1, shard_rows), F32),
        V((E * PC, HP, L), F32), V((E * PC, HP, L), F32), V((PC, HP, L), F32),
        V((max((E - 1) * PC, 1), HP, L), BF16), V((max((E - 1) * PC, 1), HP, L), BF16),
        V((max(R - 1, 1), HP, L), BF16), V((max(R - 1, 1), HP, L), BF16),
        V((E * PC, HP, L), BF16), V((1, types), F32), V((1, types), F32),
    ]
    for count in (1, E - 1, 2 * R - 1, 1, R * E - 1, E * PC, (E - 1) * PC, R - 1, R - 1, R * (E - 1), 2):
        scratch += [sem(count), sem(count)]
    vm = pl.BlockSpec(memory_space=pltpu.VMEM)
    new_ent, new_est, new_rel, new_rst = pl.pallas_call(
        functools.partial(kernel, n),
        out_shape=[
            jax.ShapeDtypeStruct((half, shard_rows), F32),
            jax.ShapeDtypeStruct((1, shard_rows), F32),
            jax.ShapeDtypeStruct((half, types), F32),
            jax.ShapeDtypeStruct((1, types), F32),
        ],
        in_specs=[vm] * 9,
        out_specs=[vm] * 4,
        scratch_shapes=scratch,
        compiler_params=pltpu.CompilerParams(
            collective_id=0, has_side_effects=True, vmem_limit_bytes=60 * 2**20
        ),
        name="complex_step",
    )(
        entities.T, entity_state.reshape(1, -1), relations.T, relation_state.reshape(1, -1),
        requests[0, :, 0], head_slot[0, 0], tail_slot[0, 0], relation_ids[0, 0], negative_slot[0, 0],
    )
    return new_ent.T, new_est.reshape(-1), new_rel.T, new_rst.reshape(-1)


def solution(mesh):
    placed = (
        P(("groups", "rows"), "cols"),
        P(("groups", "rows")),
        P("groups", "cols"),
        P("groups"),
        P(("groups", "rows"), None, "edges", None, None),
        P(("groups", "rows"), "edges", None, "cols"),
        P(("groups", "rows"), "edges", None, "cols"),
        P(("groups", "rows"), "edges", None, "cols"),
        P(("groups", "rows"), "edges", None, None),
    )
    return jax.shard_map(
        local,
        mesh=mesh,
        in_specs=placed,
        out_specs=(
            P(("groups", "rows"), "cols"),
            P(("groups", "rows")),
            P("groups", "cols"),
            P("groups"),
        ),
        check_vma=False,
    )
```

```python
import functools

import jax
import jax.numpy as jnp
from jax import lax
from jax.experimental import pallas as pl
from jax.experimental.pallas import tpu as pltpu
from jax.sharding import PartitionSpec as P

LEARNING = 0.3
F32 = jnp.float32
BF16 = jnp.bfloat16
NT = (((1,), (1,)), ((), ()))
TN = (((0,), (0,)), ((), ()))


def dot(a, b):
    return jnp.dot(a, b, preferred_element_type=F32)


def dot_nt(a, b):
    return lax.dot_general(a, b, NT, preferred_element_type=F32)


def dot_tn(a, b):
    return lax.dot_general(a, b, TN, preferred_element_type=F32)


def one_hot(start, count, ids):
    rows = lax.broadcasted_iota(jnp.int32, (count, ids.shape[1]), 0) + start
    return jnp.where(rows == ids, 1.0, 0.0).astype(BF16)


def neighbours(x):
    grouped = x.reshape(x.shape[0] // 8, 8, x.shape[1])
    after = pltpu.roll(grouped, 7, 1).reshape(x.shape)
    before = pltpu.roll(grouped, 1, 1).reshape(x.shape)
    return after, before


def positions_of(slots, k, capacity, width):
    if capacity & (capacity - 1):
        owner = lax.div(slots, jnp.full_like(slots, capacity))
    else:
        owner = lax.shift_right_logical(slots, jnp.full_like(slots, capacity.bit_length() - 1))
    return slots + owner * (width - capacity) + k * capacity


def pad_rows(x, rows):
    return jnp.concatenate([x, jnp.zeros((rows - x.shape[0], x.shape[1]), x.dtype)], axis=0)


def when(static, condition):
    if static:
        return lambda body: body()
    return pl.when(condition)


def kernel(
    n, ent, est, rel, rst, req, head, tail, rid, neg,
    new_ent, new_est, new_rel, new_rst,
    relb, entb, fetg, fet, allreq, oh_head, oh_tail, oh_rel, share, rho, rho_grads,
    slot_grad, ent_send, ent_in, grad_out, grad_in, sq_ent, sq_ent_in,
    pair_out, pair_in, pair_sum, x_out, x_in, z_out, z_in, total, sq_rel, sq_rel_in,
    s_relb, r_relb, s_req, r_req, s_fet, r_fet, s_ent, r_ent, s_grad, r_grad,
    s_pair, r_pair, s_x, r_x, s_z, r_z, s_agz, r_agz, s_agx, r_agx, s_sq, r_sq,
):
    R, E, K, PW, L, PIECES, HP = n.rows, n.edges, n.blocks, n.width, n.lanes, n.pieces, n.padded
    r, e, c = lax.axis_index("rows"), lax.axis_index("edges"), lax.axis_index("cols")
    pc = 1 - c
    half = ent.shape[0]
    full = PIECES == R

    def remote(src, dst, s_sem, r_sem, row, edge, col):
        return pltpu.make_async_remote_copy(
            src_ref=src, dst_ref=dst, send_sem=s_sem, recv_sem=r_sem,
            device_id={"rows": row, "edges": edge, "cols": col},
            device_id_type=pl.DeviceIdType.MESH,
        )

    barrier = pltpu.get_barrier_semaphore()
    for dr in range(R):
        for de in range(E):
            for dc in range(2):
                if dr or de or dc:
                    pl.semaphore_signal(
                        barrier, inc=1,
                        device_id={
                            "rows": lax.rem(r + dr, R),
                            "edges": lax.rem(e + de, E),
                            "cols": lax.rem(c + dc, 2),
                        },
                        device_id_type=pl.DeviceIdType.MESH,
                    )
    sent = []

    entb[...] = pad_rows(ent[...], HP).astype(BF16)
    relb[c] = pad_rows(rel[...], HP).astype(BF16)
    for w in range(R):
        ids = jnp.concatenate([req[w, k : k + 1, :] for k in range(K)], axis=1)
        allreq[e, :, w * PW : (w + 1) * PW] = ids
        fetg[w] = dot(entb[...], one_hot(0, ent.shape[1], ids)).astype(BF16)
    pl.semaphore_wait(barrier, R * E * 2 - 1)

    fetch = []
    for dr in range(R):
        row = lax.rem(r + dr, R)
        here = fet.at[c, :, pl.ds(pl.multiple_of(r * PW, PW), PW)]
        for dc in range(2):
            if dr or dc:
                i = dr * 2 + dc - 1
                copy = remote(fetg.at[row], here, s_fet.at[i], r_fet.at[i], row, e, lax.rem(c + dc, 2))
                copy.start()
                fetch.append(copy)
    fet[c, :, pl.ds(pl.multiple_of(r * PW, PW), PW)] = fetg[r]
    relation_copy = remote(relb.at[c], relb.at[c], s_relb.at[0], r_relb.at[0], r, e, pc)
    relation_copy.start()
    request_copies = []
    for de in range(1, E):
        copy = remote(
            allreq.at[e], allreq.at[e], s_req.at[de - 1], r_req.at[de - 1], r, lax.rem(e + de, E), c
        )
        copy.start()
        request_copies.append(copy)
    sent += fetch + [relation_copy] + request_copies

    positions = R * PW
    negatives = neg.shape[1]
    for k in range(K):
        slots = lax.broadcasted_iota(jnp.int32, (positions, 128), 0)
        hits = jnp.zeros((positions, 128), F32)
        for at in range(0, negatives, 128):
            ids = positions_of(neg[k : k + 1, at : at + 128], k, n.capacity, PW)
            hits += jnp.where(slots == ids, 1.0, 0.0)
        share[k] = jnp.sum(hits, axis=1, keepdims=True) / negatives

    per_block = head.shape[1]
    edges = K * per_block
    step = n.step
    for k in range(K):

        @pl.loop(0, per_block // step)
        def _(t):
            ids = pl.ds(pl.multiple_of(t * step, step), step)
            cols = pl.ds(pl.multiple_of(k * per_block + t * step, step), step)
            heads = positions_of(head[k : k + 1, ids], k, n.capacity, PW)
            tails = positions_of(tail[k : k + 1, ids], k, n.capacity, PW)
            oh_head[:, cols] = one_hot(0, positions, heads)
            oh_tail[:, cols] = one_hot(0, positions, tails)
            oh_rel[:, cols] = one_hot(0, rel.shape[1], rid[k : k + 1, ids])
            rho[c, :, cols] = dot(relb[c], oh_rel[:, cols]).astype(BF16)

    relation_copy.wait_recv()

    @pl.loop(0, edges // step)
    def _(t):
        cols = pl.ds(pl.multiple_of(t * step, step), step)
        rho[pc, :, cols] = dot(relb[pc], oh_rel[:, cols]).astype(BF16)

    for copy in fetch:
        copy.wait_recv()

    slot_grad[...] = jnp.zeros_like(slot_grad)
    for k in range(K):

        @pl.loop(0, per_block // step)
        def _(t):
            cols = pl.ds(pl.multiple_of(k * per_block + t * step, step), step)
            rows = fet[...].reshape(2 * HP, positions)
            h = dot(rows, oh_head[:, cols])
            tl = dot(rows, oh_tail[:, cols])
            rh = rho[:, :, cols].reshape(2 * HP, step).astype(F32)
            even = lax.rem(lax.broadcasted_iota(jnp.int32, (2 * HP, step), 0), 2) == 0
            h_after, h_before = neighbours(h)
            r_after, r_before = neighbours(rh)
            r_re = jnp.where(even, rh, r_before)
            r_im = jnp.where(even, -r_after, rh)
            query = h * r_re + jnp.where(even, h_after, h_before) * r_im
            query_b = query.astype(BF16)
            positive = jnp.sum(query * tl, axis=0, keepdims=True)
            pos_weight = -jax.nn.sigmoid(-positive)
            scores = dot_tn(rows, query_b)
            weight = (jax.nn.sigmoid(scores) * share[k]).astype(BF16)
            g = pos_weight * tl + dot(rows, weight)
            g_after, g_before = neighbours(g)
            g_swap = jnp.where(even, g_after, g_before)
            head_grad = g * r_re - g_swap * r_im
            h_re = jnp.where(even, h, h_before)
            h_im = jnp.where(even, -h_after, h)
            rho_grad = g * h_re - g_swap * h_im
            rho_grads[:, :, cols] = rho_grad.astype(BF16).reshape(2, HP, step)
            acc = dot_nt(query_b, weight)
            acc += dot_nt(head_grad.astype(BF16), oh_head[:, cols])
            acc += dot_nt((pos_weight * query).astype(BF16), oh_tail[:, cols])
            slot_grad[...] += acc.reshape(2, HP, positions)

    ent_send[...] = slot_grad[pc]
    entity_pair = remote(ent_send, ent_in, s_ent.at[0], r_ent.at[0], r, e, pc)
    entity_pair.start()
    sent.append(entity_pair)

    def place(de, p):
        piece = lax.rem(r + 1 + p, R) if full else p
        return pl.multiple_of((lax.rem(e + de, E) * PIECES + piece) * L, L)

    order = [(de, p) for de in list(range(1, E)) + [0] for p in range(PIECES)]
    pairs = {}

    def dense(which, de, p):
        hot = oh_rel[pl.ds(place(de, p), L), :]
        return dot_nt(rho_grads[which], hot)

    def send_pair(de, p):
        i = de * PIECES + p
        pair_out[i] = dense(pc, de, p)
        copy = remote(pair_out.at[i], pair_in.at[i], s_pair.at[i], r_pair.at[i], r, e, pc)
        copy.start()
        pairs[de, p] = copy
        sent.append(copy)

    def x_copy(de, p):
        i = (de - 1) * PIECES + p
        return remote(x_out.at[i], x_in.at[i], s_x.at[i], r_x.at[i], r, lax.rem(e + de, E), c)

    def entity_out():
        entity_pair.wait_recv()
        summed = (slot_grad[c] + ent_in[...]).astype(BF16)
        for o in range(R):
            grad_out[o] = summed[:, o * PW : (o + 1) * PW]
        copies = []
        for dr in range(R):
            row = lax.rem(r + dr, R)
            for de in range(E):
                if dr or de:
                    i = dr * E + de - 1
                    copy = remote(
                        grad_out.at[row],
                        grad_in.at[e, :, pl.ds(pl.multiple_of(r * PW, PW), PW)],
                        s_grad.at[i], r_grad.at[i], row, lax.rem(e + de, E), c,
                    )
                    copy.start()
                    copies.append(copy)
        grad_in[e, :, pl.ds(pl.multiple_of(r * PW, PW), PW)] = grad_out[r]
        sent.extend(copies)
        return copies

    send_pair(*order[0])
    for at, (de, p) in enumerate(order):
        if at + 1 < len(order):
            send_pair(*order[at + 1])
        own = dense(c, de, p)
        pairs[de, p].wait_recv()
        own += pair_in[de * PIECES + p]
        if de:
            x_out[(de - 1) * PIECES + p] = own.astype(BF16)
            copy = x_copy(de, p)
            copy.start()
            sent.append(copy)
        else:
            pair_sum[p] = own

    def over_edges(p):
        acc = pair_sum[p]
        for de in range(1, E):
            x_copy(de, p).wait_recv()
            acc += x_in[(de - 1) * PIECES + p].astype(F32)
        return acc

    def z_copy(dr):
        return remote(
            z_out.at[dr - 1], z_in.at[dr - 1], s_z.at[dr - 1], r_z.at[dr - 1], lax.rem(r + dr, R), e, c
        )

    for dr in range(1, R):
        p = lax.rem(r + dr, R)

        @when(full, p < PIECES)
        def _():
            z_out[dr - 1] = over_edges(dr - 1 if full else p).astype(BF16)
            z_copy(dr).start()

    grads = entity_out()

    def mine(dr):
        return e * PIECES + lax.rem(r + R - dr, R)

    def agz_copy(dr):
        return remote(
            total.at[mine(0)], total.at[mine(0)], s_agz.at[dr - 1], r_agz.at[dr - 1],
            lax.rem(r + dr, R), e, c,
        )

    def agx_copy(dr, de):
        i = dr * (E - 1) + de - 1
        return remote(
            total.at[mine(dr)], total.at[mine(dr)], s_agx.at[i], r_agx.at[i],
            r, lax.rem(e + de, E), c,
        )

    @when(full, r < PIECES)
    def _():
        acc = over_edges(R - 1 if full else r)
        for dr in range(1, R):
            z_copy(dr).wait_recv()
            acc += z_in[dr - 1].astype(F32)
        total[mine(0)] = acc.astype(BF16)
        for dr in range(1, R):
            agz_copy(dr).start()
        for de in range(1, E):
            agx_copy(0, de).start()

    for copy in request_copies + grads:
        copy.wait_recv()
    tile = n.tile

    @pl.loop(0, ent.shape[1] // tile)
    def _(t):
        cols = pl.ds(pl.multiple_of(t * tile, tile), tile)
        acc = jnp.zeros((HP, tile), F32)
        for edge in range(E):
            acc += dot_nt(grad_in[edge], one_hot(t * tile, tile, allreq[edge]))
        new_ent[:, cols] = acc[:half, :]
        sq_ent[:, cols] = jnp.sum(acc * acc, axis=0, keepdims=True)

    squares = remote(sq_ent, sq_ent_in, s_sq.at[0], r_sq.at[0], r, e, pc)
    squares.start()
    sent.append(squares)

    for dr in range(1, R):

        @when(full, lax.rem(r + R - dr, R) < PIECES)
        def _():
            agz_copy(dr).wait_recv()
            for de in range(1, E):
                agx_copy(dr, de).start()

    squares.wait_recv()
    state = est[...] + (sq_ent[...] + sq_ent_in[...]) / (2 * half)
    new_est[...] = state
    new_ent[...] = ent[...] - new_ent[...] * (LEARNING / jnp.sqrt(state))

    for dr in range(R):
        for de in range(1, E):

            @when(full, lax.rem(r + R - dr, R) < PIECES)
            def _():
                agx_copy(dr, de).wait_recv()

    for i in range(E * PIECES):
        g = total[i].astype(F32)
        sq_rel[:, i * L : (i + 1) * L] = jnp.sum(g * g, axis=0, keepdims=True)
    squares = remote(sq_rel, sq_rel_in, s_sq.at[1], r_sq.at[1], r, e, pc)
    squares.start()
    sent.append(squares)
    squares.wait_recv()
    state = rst[...] + (sq_rel[...] + sq_rel_in[...]) / (2 * half)
    new_rst[...] = state
    scale = LEARNING / jnp.sqrt(state)
    for i in range(E * PIECES):
        at = slice(i * L, (i + 1) * L)
        new_rel[:, at] = rel[:, at] - total[i].astype(F32)[:half, :] * scale[:, at]

    for copy in sent:
        copy.wait_send()
    for dr in range(1, R):

        @when(full, lax.rem(r + dr, R) < PIECES)
        def _():
            z_copy(dr).wait_send()

        @when(full, r < PIECES)
        def _():
            agz_copy(dr).wait_send()

    for dr in range(R):
        for de in range(1, E):

            @when(full, lax.rem(r + R - dr, R) < PIECES)
            def _():
                agx_copy(dr, de).wait_send()


class Sizes:
    pass


def local(
    entities, entity_state, relations, relation_state, requests,
    head_slot, tail_slot, relation_ids, negative_slot,
):
    n = Sizes()
    n.rows, n.edges = lax.axis_size("rows"), lax.axis_size("edges")
    n.blocks = requests.shape[3]
    capacity = n.capacity = requests.shape[4]
    shard_rows, half = entities.shape
    types = relations.shape[0]
    n.width = n.blocks * capacity
    n.padded = -(-half // 16) * 16
    n.lanes = -(-types // (n.rows * n.edges * 128)) * 128
    n.pieces = types // (n.edges * n.lanes)
    n.step = 256 if n.rows * n.width <= 1024 else 128
    n.tile = 256
    positions = n.rows * n.width
    edges = n.blocks * head_slot.shape[3]

    HP, R, E, PC, L = n.padded, n.rows, n.edges, n.pieces, n.lanes
    V = pltpu.VMEM
    sem = lambda k: pltpu.SemaphoreType.DMA((max(k, 1),))
    scratch = [
        V((2, HP, types), BF16), V((HP, shard_rows), BF16), V((R, HP, n.width), BF16),
        V((2, HP, positions), BF16), V((E, 1, positions), jnp.int32),
        V((positions, edges), BF16), V((positions, edges), BF16), V((types, edges), BF16),
        V((n.blocks, positions, 1), F32), V((2, HP, edges), BF16),
        V((2, HP, edges), BF16),
        V((2, HP, positions), F32), V((HP, positions), F32), V((HP, positions), F32),
        V((R, HP, n.width), BF16), V((E, HP, positions), BF16),
        V((1, shard_rows), F32), V((1, shard_rows), F32),
        V((E * PC, HP, L), F32), V((E * PC, HP, L), F32), V((PC, HP, L), F32),
        V((max((E - 1) * PC, 1), HP, L), BF16), V((max((E - 1) * PC, 1), HP, L), BF16),
        V((max(R - 1, 1), HP, L), BF16), V((max(R - 1, 1), HP, L), BF16),
        V((E * PC, HP, L), BF16), V((1, types), F32), V((1, types), F32),
    ]
    for count in (1, E - 1, 2 * R - 1, 1, R * E - 1, E * PC, (E - 1) * PC, R - 1, R - 1, R * (E - 1), 2):
        scratch += [sem(count), sem(count)]
    vm = pl.BlockSpec(memory_space=pltpu.VMEM)
    new_ent, new_est, new_rel, new_rst = pl.pallas_call(
        functools.partial(kernel, n),
        out_shape=[
            jax.ShapeDtypeStruct((half, shard_rows), F32),
            jax.ShapeDtypeStruct((1, shard_rows), F32),
            jax.ShapeDtypeStruct((half, types), F32),
            jax.ShapeDtypeStruct((1, types), F32),
        ],
        in_specs=[vm] * 9,
        out_specs=[vm] * 4,
        scratch_shapes=scratch,
        compiler_params=pltpu.CompilerParams(
            collective_id=0, has_side_effects=True, vmem_limit_bytes=60 * 2**20
        ),
        name="complex_step",
    )(
        entities.T, entity_state.reshape(1, -1), relations.T, relation_state.reshape(1, -1),
        requests[0, :, 0], head_slot[0, 0], tail_slot[0, 0], relation_ids[0, 0], negative_slot[0, 0],
    )
    return new_ent.T, new_est.reshape(-1), new_rel.T, new_rst.reshape(-1)


def solution(mesh):
    placed = (
        P(("groups", "rows"), "cols"),
        P(("groups", "rows")),
        P("groups", "cols"),
        P("groups"),
        P(("groups", "rows"), None, "edges", None, None),
        P(("groups", "rows"), "edges", None, "cols"),
        P(("groups", "rows"), "edges", None, "cols"),
        P(("groups", "rows"), "edges", None, "cols"),
        P(("groups", "rows"), "edges", None, None),
    )
    return jax.shard_map(
        local,
        mesh=mesh,
        in_specs=placed,
        out_specs=(
            P(("groups", "rows"), "cols"),
            P(("groups", "rows")),
            P("groups", "cols"),
            P("groups"),
        ),
        check_vma=False,
    )
```
